32 devices in a mesh: rep: 8 (over z, x), fsdp: 4 (over y, core).
Axes of the slice: x: 2, y: 2, z: 4, core: 2. Of those that a mesh axis runs over, the one named last changes fastest.
Arguments:
- tokens: bfloat16 [32768, 1024], P(('rep', 'fsdp')), may hold values from -6 to 6
- norm_w: bfloat16 [1024], P('fsdp'), may hold values from 0.099609375 to 1.8984375
- in_w: bfloat16 [1024, 4384], P('fsdp'), may hold values from -0.1875 to 0.1875
- conv_w: bfloat16 [4, 2304], P(None, 'fsdp'), may hold values from -3 to 3
- conv_b: bfloat16 [2304], P('fsdp'), may hold values from -0.5 to 0.5
- dt_bias: bfloat16 [32], P('fsdp'), may hold values from -2 to 0.5
- a_log: bfloat16 [32], P('fsdp'), may hold values from -8 to 0.5
- d_skip: bfloat16 [32], P('fsdp'), may hold values from 0.5 to 1.5
- gnorm_w: bfloat16 [2048], P('fsdp'), may hold values from 0.099609375 to 1.8984375
- out_w: bfloat16 [2048, 1024], P('fsdp'), may hold values from -0.125 to 0.125
- first_length: int32 [8], P('rep'), may hold values from 1024 to 3072, as said below
- cotangent: bfloat16 [32768, 1024], P(('rep', 'fsdp')), may hold values from -6 to 6
Outputs:
- output: bfloat16 [32768, 1024], P(('rep', 'fsdp'))
- d_tokens: float32 [32768, 1024], P(('rep', 'fsdp'))
- d_norm_w: float32 [1024], P('fsdp')
- d_in_w: float32 [1024, 4384], P('fsdp')
- d_conv_w: float32 [4, 2304], P(None, 'fsdp')
- d_conv_b: float32 [2304], P('fsdp')
- d_dt_bias: float32 [32], P('fsdp')
- d_a_log: float32 [32], P('fsdp')
- d_d_skip: float32 [32], P('fsdp')
- d_gnorm_w: float32 [2048], P('fsdp')
- d_out_w: float32 [2048, 1024], P('fsdp')
The draws below stay inside these ranges and needn't reach their ends.
Inputs may be any that keep to these rules, and one draw needn't show every extreme that they name: The second sequence of group g has 4096 - first_length[g] tokens; some group has each end of the range.
All inputs are finite; a program needn't handle non-finite values.
Results may differ from the reference program's by a relative error of at most 0.0061.
Values may be sent and summed in bfloat16 or wider, within the bound.
A program may use at most 256 MiB of HBM per device.

```python
import jax
import jax.numpy as jnp
from jax import lax

D = 1024
H = 32
P_SIZE = 64
N = 128
K = 4
Q = 256
MIN_LEN = 1024
E = 2048
CH = 2304
C = 4384
GROUP = 4096
GROUPS = 8
TOKENS = 32768


def draw_first_length(key, part):
    key = jax.random.fold_in(key, 7)
    subkeys = jax.random.split(key, 3)
    values = jax.random.randint(subkeys[0], (GROUPS,), MIN_LEN, GROUP - MIN_LEN + 1)
    high_at = jax.random.randint(subkeys[1], (), 0, GROUPS)
    low_at = (high_at + jax.random.randint(subkeys[2], (), 1, GROUPS)) % GROUPS
    places = jnp.arange(GROUPS)
    values = jnp.where(places == high_at, GROUP - MIN_LEN, values)
    values = jnp.where(places == low_at, MIN_LEN, values)
    return values.astype(jnp.int32)


def block_scale(stream_key, extent, cuts, smallest, top_value):
    level, own = 1.0, jax.random.fold_in(stream_key, 6)
    for axis_at, parts in cuts:
        draws = jnp.exp(jax.random.uniform(jax.random.fold_in(own, axis_at), (parts,), jnp.float32, smallest / len(cuts), top_value / len(cuts)))
        level = level * jnp.repeat(draws, extent[axis_at] // parts).reshape([-1 if axis == axis_at else 1 for axis in range(len(extent))])
    return level


def noise(rng, shape, scale, most, cuts=(), kind=jnp.bfloat16):
    values = jax.random.normal(rng, shape, jnp.float32) * scale
    if len(cuts) > 0:
        values = block_scale(rng, shape, cuts, -0.22, 0.18) * values
    return jnp.clip(values, min=-most, max=most).astype(kind)


def setup_inputs(seed: int = 0) -> dict:
    keys = jax.random.split(jax.random.key(seed), 13)
    tokens = noise(keys[0], (TOKENS, D), 1.0, 6.0, ((0, 32),))
    norm_w = jnp.clip(1.0 + 0.18 * jax.random.normal(keys[1], (D,), jnp.float32), 0.099609375, 1.8984375).astype(jnp.bfloat16)
    in_w = noise(keys[2], (D, C), D ** -0.5, 0.1875, ((0, 4),))
    conv_w = noise(keys[3], (K, CH), 0.5, 3.0, ((1, 4),))
    conv_b = jnp.clip(jax.random.uniform(keys[4], (CH,), jnp.float32, -0.5, 0.5) * block_scale(keys[4], (CH,), ((0, 4),), -0.4, 0.0), -0.5, 0.5).astype(jnp.bfloat16)
    dt_bias = jnp.clip(-2.0 + 2.5 * jax.random.uniform(keys[5], (H,), jnp.float32) ** block_scale(keys[5], (H,), ((0, 4),), -0.2, 0.2), -2.0, 0.5).astype(jnp.bfloat16)
    a_log = jnp.clip(-8.0 + 8.5 * jax.random.uniform(keys[6], (H,), jnp.float32) ** block_scale(keys[6], (H,), ((0, 4),), -0.2, 0.2), -8.0, 0.5).astype(jnp.bfloat16)
    d_skip = jnp.clip(0.5 + 1.0 * jax.random.uniform(keys[7], (H,), jnp.float32) ** block_scale(keys[7], (H,), ((0, 4),), -0.2, 0.2), 0.5, 1.5).astype(jnp.bfloat16)
    gnorm_w = jnp.clip(1.0 + 0.18 * jax.random.normal(keys[8], (E,), jnp.float32), 0.099609375, 1.8984375).astype(jnp.bfloat16)
    out_w = noise(keys[9], (E, D), E ** -0.5, 0.125, ((0, 4),))
    first_length = draw_first_length(jax.random.fold_in(keys[12], 71), 0)
    cotangent = noise(keys[11], (TOKENS, D), 1.0, 6.0, ((0, 32),))
    return {"tokens": tokens, "norm_w": norm_w, "in_w": in_w, "conv_w": conv_w, "conv_b": conv_b, "dt_bias": dt_bias, "a_log": a_log, "d_skip": d_skip, "gnorm_w": gnorm_w, "out_w": out_w, "first_length": first_length, "cotangent": cotangent}


highest = lax.Precision.HIGHEST
epsilon = 1e-05

@jax.custom_vjp
def low(v):
    return lax.optimization_barrier(v.astype(jnp.bfloat16)).astype(jnp.float32)

@jax.custom_vjp
def low_back(v):
    return v

def low_keep(v):
    return (low(v), None)

def low_pass(kept, grad):
    return (grad,)

def back_keep(v):
    return (v, None)

def back_low(kept, grad):
    return (low(grad),)
low.defvjp(low_keep, low_pass)
low_back.defvjp(back_keep, back_low)

def rms_scale(values):
    return values * lax.rsqrt(lax.optimization_barrier(jnp.mean(values * values, axis=-1, keepdims=True)) + epsilon)

def gate_norm(result, z_part, gain):
    return rms_scale(result * jax.nn.silu(z_part)) * gain

def convolve(full, conv_w, conv_b, places, starts):
    taps = conv_w.shape[0]
    length = places.shape[0]
    total = jnp.zeros((length, full.shape[1]), jnp.float32) + conv_b[None, :]
    for index in range(taps):
        source = (places - (taps - 1) + index).astype(jnp.int32)
        valid = (source >= starts).astype(jnp.float32)
        total = total + full[index:index + length] * conv_w[index][None, :] * valid[:, None]
    return jax.nn.silu(total)

def span_step(state, pieces):
    xs_part, delta, bmat, cmat, decay, segment, seg_prev = pieces
    cumul = jnp.cumsum(decay, axis=0)
    count = segment.shape[0]
    spots = jnp.arange(count, dtype=jnp.int32)
    causal = (spots[:, None] >= spots[None, :]) & (segment[:, None] == segment[None, :])
    spread = cumul.T[:, :, None] - cumul.T[:, None, :]
    weights = jnp.exp(jnp.where(causal[None], spread, jnp.zeros_like(spread))) * causal[None].astype(jnp.float32)
    inner = jnp.dot(cmat, bmat.T, precision=highest, preferred_element_type=jnp.float32)
    mixing = weights * inner[None] * delta.T[:, None, :]
    intra = jnp.einsum('hts,shp->thp', mixing, xs_part, precision=highest)
    carried = (segment == seg_prev).astype(jnp.float32)
    entry = jnp.exp(cumul) * carried[:, None]
    from_state = jnp.einsum('tn,hpn->thp', cmat, state, precision=highest) * entry[:, :, None]
    last_seg = segment[-1]
    tail = jnp.exp(cumul[-1][None, :] - cumul) * (segment == last_seg).astype(jnp.float32)[:, None] * delta
    keep_old = jnp.exp(cumul[-1]) * (last_seg == seg_prev).astype(jnp.float32)
    new_state = state * keep_old[:, None, None] + jnp.einsum('sh,shp,sn->hpn', tail, xs_part, bmat, precision=highest)
    return (new_state, intra + from_state)

def scan_spans(xs_all, delta, bmat, cmat, decay, segment, seg_before):
    count = xs_all.shape[0] // Q

    def split_up(values):
        return values.reshape((count, Q) + values.shape[1:])
    seg_blocks = split_up(segment.astype(jnp.int32))
    seg_prev = jnp.concatenate([jnp.reshape(seg_before.astype(jnp.int32), (1,)), seg_blocks[:-1, -1].astype(jnp.int32)]).astype(jnp.int32)
    zero_state = jnp.zeros((H, P_SIZE, N), jnp.float32)
    final, pieces = lax.scan(jax.checkpoint(span_step), zero_state, (split_up(xs_all), split_up(delta), split_up(bmat), split_up(cmat), split_up(decay), seg_blocks, seg_prev))
    return (final, pieces.reshape(xs_all.shape))

def ssm_inputs(proj, rim_rows, conv_w, conv_b, dt_bias, a_log, d_skip, places, starts, segment, seg_before):
    length = proj.shape[0]
    xbc = proj[:, E:2 * E + 2 * N]
    full = jnp.concatenate([rim_rows, xbc], axis=0)
    mixed = convolve(full, conv_w, conv_b, places, starts)
    xs_all = mixed[:, :E].reshape(length, H, P_SIZE)
    bmat = mixed[:, E:E + N]
    cmat = mixed[:, E + N:]
    delta = jax.nn.softplus(proj[:, 2 * E + 2 * N:] + dt_bias[None, :])
    decay = -jnp.exp(a_log)[None, :] * delta
    final, result = scan_spans(xs_all, delta, bmat, cmat, decay, segment, seg_before)
    result = result + d_skip[None, :, None] * xs_all
    return (result, cmat, decay, final)

def layer(tokens, norm_w, in_w, conv_w, conv_b, dt_bias, a_log, d_skip, gnorm_w, out_w, first_length):
    places = jnp.arange(GROUP, dtype=jnp.int32)

    def one_group(carry, pieces):
        inputs_f, boundary_in = pieces
        boundary = boundary_in.astype(jnp.int32)
        starts = jnp.where(places >= boundary, boundary, jnp.zeros_like(boundary)).astype(jnp.int32)
        segment = (places >= boundary).astype(jnp.int32)
        normed = low(rms_scale(inputs_f) * norm_w[None, :])
        proj = low_back(jnp.dot(normed, in_w, precision=highest, preferred_element_type=jnp.float32))
        rim_rows = jnp.zeros((K - 1, E + 2 * N), jnp.float32)
        result, cmat, decay, final = ssm_inputs(proj, rim_rows, conv_w, conv_b, dt_bias, a_log, d_skip, places, starts, segment, jnp.zeros((), jnp.int32))
        gated = low(gate_norm(result.reshape(GROUP, E), proj[:, :E], gnorm_w[None, :]))
        branch = jnp.dot(gated, out_w, precision=highest, preferred_element_type=jnp.float32)
        return (carry, inputs_f + branch)
    zero_carry = jnp.zeros((), jnp.float32)
    _, outputs = lax.scan(one_group, zero_carry, (tokens.reshape(GROUPS, GROUP, D), first_length.astype(jnp.int32)))
    return outputs.reshape(GROUPS * GROUP, D)

def reference(tokens, norm_w, in_w, conv_w, conv_b, dt_bias, a_log, d_skip, gnorm_w, out_w, first_length, cotangent):
    primal = tuple((value.astype(jnp.float32) for value in (tokens, norm_w, in_w, conv_w, conv_b, dt_bias, a_log, d_skip, gnorm_w, out_w)))

    def forward(*values):
        return layer(*values, first_length)
    output, pull = jax.vjp(forward, *primal)
    grads = pull(cotangent.astype(jnp.float32))
    return (output.astype(jnp.bfloat16), grads[0], grads[1], grads[2], grads[3], grads[4], grads[5], grads[6], grads[7], grads[8], grads[9])
```

```python
import jax
import jax.numpy as jnp
from jax import lax
from jax.sharding import PartitionSpec as P

H = 32
P_SIZE = 64
N = 128
E = 2048
CHUNK = 128
RESET = 128.0

highest = lax.Precision.HIGHEST
epsilon = 1e-05
low = jnp.bfloat16
wide = jnp.float32


def shifted(x, axis, by):
    peers = lax.axis_size(axis)
    pairs = [(i, i + by) for i in range(peers) if 0 <= i + by < peers]
    return lax.ppermute(x, axis, pairs)


def swapped(x, axis, bit):
    return lax.ppermute(x, axis, [(i, i ^ bit) for i in range(lax.axis_size(axis))])


def mm(spec, a, b):
    return jnp.einsum(spec, a.astype(low), b.astype(low), preferred_element_type=wide)


def exact(spec, a, b):
    return jnp.einsum(spec, a, b, precision=highest, preferred_element_type=wide)


def gather_rows(x, axis):
    count, me = lax.axis_size(axis), lax.axis_index(axis)
    held = x[None]
    bit = count // 2
    while bit >= 1:
        other = swapped(held, axis, bit)
        mine_first = (me & bit) == 0
        pair = jnp.stack(
            [jnp.where(mine_first, held, other), jnp.where(mine_first, other, held)], axis=1
        )
        held = pair.reshape((-1,) + x.shape)
        bit //= 2
    return held.reshape((count * x.shape[0],) + x.shape[1:])


def reduce_rows(partial):
    owners, mine = lax.axis_size("fsdp"), lax.axis_index("fsdp")
    held = partial.reshape((owners, partial.shape[0] // owners) + partial.shape[1:])
    bit = 1
    while bit < owners:
        pair = held.reshape((held.shape[0] // 2, 2) + held.shape[1:])
        side = (mine // bit) % 2
        keep = lax.dynamic_index_in_dim(pair, side, 1, False)
        send = lax.dynamic_index_in_dim(pair, 1 - side, 1, False).astype(low)
        held = keep + swapped(send, "fsdp", bit).astype(wide)
        bit *= 2
    held = held[0]
    copies, here = lax.axis_size("rep"), lax.axis_index("rep")
    bit = 1
    while bit < copies:
        half = held.shape[0] // 2
        side = (here // bit) % 2
        keep = lax.dynamic_slice_in_dim(held, side * half, half, 0)
        send = lax.dynamic_slice_in_dim(held, (1 - side) * half, half, 0).astype(low)
        held = keep + swapped(send, "rep", bit).astype(wide)
        bit *= 2
    held = held.astype(low)
    while bit > 1:
        bit //= 2
        other = swapped(held, "rep", bit)
        lower = ((here // bit) % 2) == 0
        held = jnp.concatenate(
            [jnp.where(lower, held, other), jnp.where(lower, other, held)], axis=0
        )
    return held.astype(wide)


def silu_parts(x):
    s = jax.nn.sigmoid(x)
    return x * s, s * (1.0 + x * (1.0 - s))


def body(
    tokens,
    norm_w,
    in_w,
    conv_w,
    conv_b,
    dt_bias,
    a_log,
    d_skip,
    gnorm_w,
    out_w,
    first_length,
    cotangent,
):
    ranks, rank = lax.axis_size("fsdp"), lax.axis_index("fsdp")
    length = tokens.shape[0]
    count = length // CHUNK
    taps = conv_w.shape[0]
    smalls = (norm_w, conv_w.T, conv_b, dt_bias, a_log, d_skip, gnorm_w)
    flat = lax.all_gather(jnp.concatenate([v.reshape(-1) for v in smalls]), "fsdp", axis=0)
    flat = flat.astype(wide)
    parts, at = [], 0
    for v in smalls:
        parts.append(flat[:, at : at + v.size].reshape((ranks * v.shape[0],) + v.shape[1:]))
        at += v.size
    norm32, conv32, bias32, dt32, alog32, skip32, gnorm32 = parts
    conv32 = conv32.T
    w_x = gather_rows(in_w[:, E:], "fsdp")
    in_z, out_s, w_x = lax.optimization_barrier((in_w[:, :E], out_w, w_x))
    w_z = gather_rows(in_z, "fsdp")
    w_out = gather_rows(out_s, "fsdp")

    first_place = rank * length
    places = first_place + jnp.arange(length + taps - 1, dtype=jnp.int32)
    boundary = first_length[0]
    starts = jnp.where(places >= boundary, boundary, jnp.zeros_like(boundary))

    def tap_valid(index, lo, hi):
        ok = places[lo:hi] - (taps - 1) + index >= starts[lo:hi]
        return ok.astype(wide)[:, None]

    u = tokens.astype(wide)
    scale_in = lax.rsqrt(jnp.mean(u * u, axis=-1, keepdims=True) + epsilon)
    normed = (u * scale_in * norm32[None, :]).astype(low)
    proj_x = jnp.dot(normed, w_x, preferred_element_type=wide)
    xbc = proj_x[:, : E + 2 * N]
    rim = shifted(xbc[length - (taps - 1) :], "fsdp", 1)

    full = jnp.concatenate([rim, xbc], axis=0)
    pre = jnp.zeros_like(xbc) + bias32[None, :]
    for k in range(taps):
        pre = pre + full[k : k + length] * conv32[k][None, :] * tap_valid(k, 0, length)
    xc = pre * jax.nn.sigmoid(pre)

    draw = proj_x[:, E + 2 * N :] + dt32[None, :]
    delta_rows = jax.nn.softplus(draw)
    reset = RESET * (places[:length] == boundary).astype(wide)
    rate = -jnp.exp(alog32)

    def by_head(v):
        return v.reshape(count, CHUNK, H).transpose(0, 2, 1)

    delta = by_head(delta_rows)
    decay = delta * rate[None, :, None] - reset.reshape(count, 1, CHUNK)
    spots = jnp.arange(CHUNK)
    upto = (spots[:, None] <= spots[None, :]).astype(wide)
    cum = exact("chs,st->cht", decay, upto)
    last = cum[:, :, -1]
    growth = jnp.exp(last)
    totals = lax.all_gather(jnp.exp(jnp.sum(last, axis=0)), "fsdp", axis=0)
    entry = jnp.exp(cum)[:, :, None, :]
    tail = jnp.exp(last[:, :, None] - cum)[:, :, None, :]

    def heads(v):
        return v.reshape(count, H, P_SIZE, CHUNK)

    def flatten(v):
        return v.reshape(count, E, CHUNK)

    def turned(v):
        return heads(v.reshape(count, CHUNK, E).transpose(0, 2, 1))

    def turned_back(v):
        return flatten(v).transpose(0, 2, 1).reshape(length, E)

    x = turned(xc[:, :E])
    bmat = xc[:, E : E + N].reshape(count, CHUNK, N)
    cmat = xc[:, E + N :].reshape(count, CHUNK, N)
    xd = x * delta[:, :, None, :]
    xd_low = xd.astype(low)
    xw = (xd * tail).astype(low)
    state_own = mm("ceq,cqn->cen", flatten(xw), bmat).reshape(count, H, P_SIZE, N)

    def widen(v):
        return v[:, None, None]

    entering = [jnp.zeros((H, P_SIZE, N), wide)]
    before = [jnp.ones((H,), wide)]
    for c in range(count):
        entering.append(entering[c] * widen(growth[c]) + state_own[c])
        before.append(before[c] * growth[c])
    final = entering[count].astype(low)

    def incoming(value, sign):
        total, factor = jnp.zeros(value.shape, wide), jnp.ones((H,), wide)
        for j in range(1, ranks):
            got = shifted(value, "fsdp", sign * j).astype(wide)
            total = total + got * widen(factor)
            source = jnp.clip(rank - sign * j, 0, ranks - 1)
            factor = factor * lax.dynamic_index_in_dim(totals, source, 0, False)
        return total

    inflow = incoming(final, 1)
    state = jnp.stack([entering[c] + inflow * widen(before[c]) for c in range(count)])

    inner = exact("ctn,csn->cts", cmat, bmat)
    causal = (spots[:, None] >= spots[None, :])[None, None]
    spread = jnp.where(causal, cum[:, :, :, None] - cum[:, :, None, :], -1e30)
    fade = jnp.exp(spread)
    mixing = (fade * inner[:, None]).astype(low)
    state_low = state.astype(low).reshape(count, E, N)
    from_state = heads(mm("cen,ctn->cet", state_low, cmat)) * entry
    y_t = (
        mm("chps,chts->chpt", xd_low, mixing)
        + from_state
        + x * skip32[None, :, None, None]
    )
    y = turned_back(y_t)

    z = jnp.dot(normed, w_z, preferred_element_type=wide)
    silu_z, slope_z = silu_parts(z)
    g = y * silu_z
    scale_g = lax.rsqrt(jnp.mean(g * g, axis=-1, keepdims=True) + epsilon)
    hat = g * scale_g
    gated = (hat * gnorm32[None, :]).astype(low)
    output = (u + jnp.dot(gated, w_out, preferred_element_type=wide)).astype(low)

    d_gated = jnp.dot(cotangent, w_out.T, preferred_element_type=wide)
    d_out_w = reduce_rows(mm("te,td->ed", gated, cotangent))
    d_gnorm = jnp.sum(d_gated * hat, axis=0)
    d_hat = d_gated * gnorm32[None, :]
    d_g = scale_g * (d_hat - hat * jnp.mean(d_hat * hat, axis=-1, keepdims=True))
    d_y = d_g * silu_z
    d_z = (d_g * y * slope_z).astype(low)
    d_in_z = reduce_rows(mm("td,te->de", normed, d_z))

    dy = turned(d_y)
    dy_low = dy.astype(low)
    d_skip_own = jnp.sum(x * dy, axis=(0, 2, 3))
    faded = (dy * entry).astype(low)
    direct = mm("cet,ctn->cen", flatten(faded), cmat).reshape(count, H, P_SIZE, N)
    leaving = [None] * count + [jnp.zeros((H, P_SIZE, N), wide)]
    after = [None] * count + [jnp.ones((H,), wide)]
    for c in reversed(range(count)):
        leaving[c] = leaving[c + 1] * widen(growth[c]) + direct[c]
        after[c] = after[c + 1] * growth[c]
    outflow = incoming(leaving[0].astype(low), -1)
    d_state = jnp.stack([leaving[c + 1] + outflow * widen(after[c + 1]) for c in range(count)])
    d_state_low = d_state.astype(low).reshape(count, E, N)

    d_mix = mm("chpt,chps->chts", dy_low, xd_low) * fade
    d_inner = jnp.sum(d_mix, axis=1)
    weight = d_mix * inner[:, None]
    d_cum = jnp.sum(weight, axis=3) - jnp.sum(weight, axis=2) + jnp.sum(dy * from_state, axis=2)
    pulled = heads(mm("cen,cqn->ceq", d_state_low, bmat)) * tail
    d_xd = mm("chts,chpt->chps", mixing, dy_low) + pulled
    d_tail = jnp.sum(xd * pulled, axis=2)
    d_keep = growth * jnp.sum(state * d_state, axis=(2, 3))
    d_decay = (
        exact("cht,st->chs", d_cum, upto)
        + exact("chs,st->cht", d_tail, upto - jnp.eye(CHUNK, dtype=wide))
        + d_keep[:, :, None]
    )
    d_delta = jnp.sum(x * d_xd, axis=2) + d_decay * rate[None, :, None]
    d_alog = jnp.sum(d_decay * delta, axis=(0, 2)) * rate
    d_x = turned_back(d_xd * delta[:, :, None, :] + dy * skip32[None, :, None, None])
    d_c = mm("cts,csn->ctn", d_inner, bmat) + mm("cet,cen->ctn", flatten(faded), state_low)
    d_b = mm("cts,ctn->csn", d_inner, cmat) + mm("ceq,cen->cqn", flatten(xw), d_state_low)
    d_draw = d_delta.transpose(0, 2, 1).reshape(length, H) * jax.nn.sigmoid(draw)
    d_dt = jnp.sum(d_draw, axis=0)

    d_xc = jnp.concatenate([d_x, d_b.reshape(length, N), d_c.reshape(length, N)], axis=1)
    d_pre = d_xc * silu_parts(pre)[1]
    d_rim = shifted(d_pre[: taps - 1], "fsdp", -1)
    d_bias = jnp.sum(d_pre, axis=0)
    d_conv = jnp.stack(
        [
            jnp.sum(d_pre * tap_valid(k, 0, length) * full[k : k + length], axis=0)
            for k in range(taps)
        ]
    )
    d_full = jnp.concatenate([d_pre, d_rim], axis=0)
    d_xbc = jnp.zeros_like(xbc)
    for k in range(taps):
        lo = taps - 1 - k
        d_xbc = d_xbc + d_full[lo : lo + length] * conv32[k][None, :] * tap_valid(
            k, lo, lo + length
        )
    d_proj_x = jnp.concatenate([d_xbc.astype(low), d_draw.astype(low)], axis=1)
    d_in_x = reduce_rows(mm("td,te->de", normed, d_proj_x))
    d_normed = mm("te,de->td", d_z, w_z) + mm("te,de->td", d_proj_x, w_x)
    hat_in = u * scale_in
    d_norm = jnp.sum(d_normed * hat_in, axis=0)
    d_hat_in = d_normed * norm32[None, :]
    d_tokens = cotangent.astype(wide) + scale_in * (
        d_hat_in - hat_in * jnp.mean(d_hat_in * hat_in, axis=-1, keepdims=True)
    )

    owned = (d_norm, d_conv.T, d_bias, d_dt, d_alog, d_skip_own, d_gnorm)
    stacked = jnp.concatenate([v.reshape(ranks, -1) for v in owned], axis=1)
    summed = lax.psum(stacked, ("rep", "fsdp"))
    mine = lax.dynamic_index_in_dim(summed, rank, 0, False)
    grads, at = [], 0
    for v in smalls:
        grads.append(mine[at : at + v.size].reshape(v.shape))
        at += v.size
    g_norm, g_conv, g_bias, g_dt, g_alog, g_skip, g_gnorm = grads
    return (
        output,
        d_tokens,
        g_norm,
        jnp.concatenate([d_in_z, d_in_x], axis=1),
        g_conv.T,
        g_bias,
        g_dt,
        g_alog,
        g_skip,
        g_gnorm,
        d_out_w,
    )


def solution(mesh):
    in_specs = (
        P(("rep", "fsdp"), None),
        P("fsdp"),
        P("fsdp", None),
        P(None, "fsdp"),
        P("fsdp"),
        P("fsdp"),
        P("fsdp"),
        P("fsdp"),
        P("fsdp"),
        P("fsdp", None),
        P("rep"),
        P(("rep", "fsdp"), None),
    )
    out_specs = (
        P(("rep", "fsdp"), None),
        P(("rep", "fsdp"), None),
        P("fsdp"),
        P("fsdp", None),
        P(None, "fsdp"),
        P("fsdp"),
        P("fsdp"),
        P("fsdp"),
        P("fsdp"),
        P("fsdp"),
        P("fsdp", None),
    )
    return jax.shard_map(body, mesh=mesh, in_specs=in_specs, out_specs=out_specs, check_vma=False)
```

```python
import jax
import jax.numpy as jnp
from jax import lax
from jax.experimental.layout import Layout, with_layout_constraint
from jax.sharding import PartitionSpec as P

H = 32
P_SIZE = 64
N = 128
E = 2048
CHUNK = 128
RESET = 128.0

highest = lax.Precision.HIGHEST
epsilon = 1e-05
low = jnp.bfloat16
wide = jnp.float32


def shifted(x, axis, by):
    peers = lax.axis_size(axis)
    pairs = [(i, i + by) for i in range(peers) if 0 <= i + by < peers]
    return lax.ppermute(x, axis, pairs)


def pinned(v):
    return with_layout_constraint(v, Layout(major_to_minor=tuple(range(v.ndim))))


def swapped(x, axis, bit):
    return lax.ppermute(x, axis, [(i, i ^ bit) for i in range(lax.axis_size(axis))])


def mm(spec, a, b):
    return jnp.einsum(spec, a.astype(low), b.astype(low), preferred_element_type=wide)


def exact(spec, a, b):
    return jnp.einsum(spec, a, b, precision=highest, preferred_element_type=wide)


def gather_rows(x, axis):
    count, me = lax.axis_size(axis), lax.axis_index(axis)
    held = x[None]
    bit = count // 2
    while bit >= 1:
        other = swapped(held, axis, bit)
        mine_first = (me & bit) == 0
        pair = jnp.stack(
            [jnp.where(mine_first, held, other), jnp.where(mine_first, other, held)], axis=1
        )
        held = pair.reshape((-1,) + x.shape)
        bit //= 2
    return held.reshape((count * x.shape[0],) + x.shape[1:])


def owner_stages(held):
    owners, mine = lax.axis_size("fsdp"), lax.axis_index("fsdp")
    bit = 1
    while bit < owners:
        pair = held.reshape((held.shape[0] // 2, 2) + held.shape[1:])
        side = (mine // bit) % 2
        keep = lax.dynamic_index_in_dim(pair, side, 1, False)
        send = lax.dynamic_index_in_dim(pair, 1 - side, 1, False).astype(low)
        held = yield keep + swapped(send, "fsdp", bit).astype(wide)
        bit *= 2
    return held[0]


def rep_bits(last_first):
    bits, bit = [], 1
    while bit < lax.axis_size("rep"):
        bits.append(bit)
        bit *= 2
    return bits[1:] + bits[:1] if last_first else bits


def sum_stages(partial, last_first):
    owners = lax.axis_size("fsdp")
    held = partial.reshape((owners, partial.shape[0] // owners) + partial.shape[1:])
    held = yield from owner_stages(held)
    here, bits = lax.axis_index("rep"), rep_bits(last_first)
    for bit in bits:
        half = held.shape[0] // 2
        side = (here // bit) % 2
        keep = lax.dynamic_slice_in_dim(held, side * half, half, 0)
        send = lax.dynamic_slice_in_dim(held, (1 - side) * half, half, 0).astype(low)
        held = yield keep + swapped(send, "rep", bit).astype(wide)
    held = held.astype(low)
    for bit in reversed(bits):
        other = swapped(held, "rep", bit)
        lower = ((here // bit) % 2) == 0
        held = yield jnp.concatenate(
            [jnp.where(lower, held, other), jnp.where(lower, other, held)], axis=0
        )


class Reduction:
    def __init__(self, partial, last_first=False):
        self.stages = sum_stages(partial, last_first)
        self.value = next(self.stages)
        self.done = False

    def advance(self):
        if not self.done:
            try:
                self.value = self.stages.send(self.value)
            except StopIteration:
                self.done = True

    def finish(self):
        while not self.done:
            self.advance()
        return self.value.astype(wide)


def beside(value, *running):
    tied = lax.optimization_barrier((value,) + tuple(r.value for r in running))
    for r, held in zip(running, tied[1:]):
        r.value = held
        r.advance()
    return tied[0]


def sum_small(held):
    owners, mine = lax.axis_size("fsdp"), lax.axis_index("fsdp")
    bit = 1
    while bit < owners:
        pair = held.reshape((held.shape[0] // 2, 2) + held.shape[1:])
        side = (mine // bit) % 2
        keep = lax.dynamic_index_in_dim(pair, side, 1, False)
        send = lax.dynamic_index_in_dim(pair, 1 - side, 1, False)
        held = keep + swapped(send, "fsdp", bit)
        bit *= 2
    held = held[0]
    for bit in rep_bits(False):
        held = held + swapped(held, "rep", bit)
    return held


def silu_parts(x):
    s = jax.nn.sigmoid(x)
    return x * s, s * (1.0 + x * (1.0 - s))


def body(
    tokens,
    norm_w,
    in_w,
    conv_w,
    conv_b,
    dt_bias,
    a_log,
    d_skip,
    gnorm_w,
    out_w,
    first_length,
    cotangent,
):
    ranks, rank = lax.axis_size("fsdp"), lax.axis_index("fsdp")
    length = tokens.shape[0]
    count = length // CHUNK
    taps = conv_w.shape[0]
    mixed = E + 2 * N
    in_dt = in_w[:, E + mixed :]
    smalls = (norm_w, conv_w.T, conv_b, dt_bias, a_log, d_skip, gnorm_w, in_dt)
    flat = gather_rows(jnp.concatenate([v.reshape(-1) for v in smalls])[None], "fsdp")
    flat = flat.astype(wide)
    parts, at = [], 0
    for v in smalls:
        parts.append(flat[:, at : at + v.size].reshape((ranks * v.shape[0],) + v.shape[1:]))
        at += v.size
    norm32, conv32, bias32, dt32, alog32, skip32, gnorm32, w_dt = parts
    w_dt = w_dt.astype(low)
    conv32 = conv32.T
    w_x = gather_rows(in_w[:, E : E + mixed], "fsdp")
    in_z, out_s, w_x = lax.optimization_barrier((in_w[:, :E], out_w, w_x))
    w_z = gather_rows(in_z, "fsdp")
    w_out = gather_rows(out_s, "fsdp")

    first_place = rank * length
    places = first_place + jnp.arange(length + taps - 1, dtype=jnp.int32)
    boundary = first_length[0]
    starts = jnp.where(places >= boundary, boundary, jnp.zeros_like(boundary))

    def tap_valid(index, lo, hi):
        ok = places[lo:hi] - (taps - 1) + index >= starts[lo:hi]
        return ok.astype(wide)[:, None]

    u = tokens.astype(wide)
    scale_in = lax.rsqrt(jnp.mean(u * u, axis=-1, keepdims=True) + epsilon)
    normed = (u * scale_in * norm32[None, :]).astype(low)
    xbc = jnp.dot(normed, w_x, preferred_element_type=wide)
    rim = shifted(xbc[length - (taps - 1) :], "fsdp", 1)

    full = jnp.concatenate([rim, xbc], axis=0)
    pre = jnp.zeros_like(xbc) + bias32[None, :]
    for k in range(taps):
        pre = pre + full[k : k + length] * conv32[k][None, :] * tap_valid(k, 0, length)
    xc = pre * jax.nn.sigmoid(pre)

    draw = jnp.dot(normed, w_dt, preferred_element_type=wide) + dt32[None, :]
    delta_rows = jax.nn.softplus(draw)
    reset = RESET * (places[:length] == boundary).astype(wide)
    rate = -jnp.exp(alog32)

    def by_head(v):
        return v.reshape(count, CHUNK, H).transpose(0, 2, 1)

    delta = by_head(delta_rows)
    decay = delta * rate[None, :, None] - reset.reshape(count, 1, CHUNK)
    spots = jnp.arange(CHUNK)
    upto = (spots[:, None] <= spots[None, :]).astype(wide)
    cum = exact("chs,st->cht", decay, upto)
    last = cum[:, :, -1]
    growth = jnp.exp(last)
    own_total = jnp.exp(jnp.sum(last, axis=0))
    entry = jnp.exp(cum)[:, :, None, :]
    tail = jnp.exp(last[:, :, None] - cum)[:, :, None, :]

    def heads(v):
        return v.reshape(count, H, P_SIZE, CHUNK)

    def flatten(v):
        return v.reshape(count, E, CHUNK)

    def turned(v):
        return heads(v.reshape(count, CHUNK, E).transpose(0, 2, 1))

    def turned_back(v):
        return flatten(v).transpose(0, 2, 1).reshape(length, E)

    x = pinned(turned(xc[:, :E]))
    bmat = xc[:, E : E + N].reshape(count, CHUNK, N)
    cmat = xc[:, E + N :].reshape(count, CHUNK, N)
    xd = x * delta[:, :, None, :]
    xd_low = xd.astype(low)
    xw = pinned((xd * tail).astype(low))
    state_own = mm("ceq,cqn->cen", flatten(xw), bmat).reshape(count, H, P_SIZE, N)

    def widen(v):
        return v[:, None, None]

    entering = [jnp.zeros((H, P_SIZE, N), wide)]
    before = [jnp.ones((H,), wide)]
    for c in range(count):
        entering.append(entering[c] * widen(growth[c]) + state_own[c])
        before.append(before[c] * growth[c])
    final = entering[count].astype(low)

    def incoming(value, sign):
        total, factor = jnp.zeros(value.shape, wide), jnp.ones((H,), wide)
        for j in range(1, ranks):
            got = shifted(value, "fsdp", sign * j).astype(wide)
            total = total + got * widen(factor)
            if j < ranks - 1:
                factor = factor * shifted(own_total, "fsdp", sign * j)
        return total

    inflow = incoming(final, 1)
    state = jnp.stack([entering[c] + inflow * widen(before[c]) for c in range(count)])

    inner = exact("ctn,csn->cts", cmat, bmat)
    causal = (spots[:, None] >= spots[None, :])[None, None]
    spread = jnp.where(causal, cum[:, :, :, None] - cum[:, :, None, :], -1e30)
    fade = jnp.exp(spread)
    mixing = (fade * inner[:, None]).astype(low)
    state_low = state.astype(low).reshape(count, E, N)
    from_state = heads(mm("cen,ctn->cet", state_low, cmat)) * entry
    y_t = (
        mm("chps,chts->chpt", xd_low, mixing)
        + from_state
        + x * skip32[None, :, None, None]
    )
    y = turned_back(pinned(y_t))

    z = jnp.dot(normed, w_z, preferred_element_type=wide)
    silu_z, slope_z = silu_parts(z)
    g = y * silu_z
    scale_g = lax.rsqrt(jnp.mean(g * g, axis=-1, keepdims=True) + epsilon)
    hat = g * scale_g
    gated = (hat * gnorm32[None, :]).astype(low)
    output = (u + jnp.dot(gated, w_out, preferred_element_type=wide)).astype(low)

    d_gated = jnp.dot(cotangent, w_out.T, preferred_element_type=wide)
    sum_out = Reduction(mm("te,td->ed", gated, cotangent))
    d_gnorm = jnp.sum(d_gated * hat, axis=0)
    d_hat = d_gated * gnorm32[None, :]
    d_g = scale_g * (d_hat - hat * jnp.mean(d_hat * hat, axis=-1, keepdims=True))
    d_y = d_g * silu_z
    d_z = (d_g * y * slope_z).astype(low)
    sum_z = Reduction(mm("td,te->de", normed, d_z), True)
    d_y = beside(d_y, sum_out)

    dy = pinned(turned(d_y))
    dy = beside(dy, sum_z)
    dy_low = dy.astype(low)
    d_skip_own = jnp.sum(x * dy, axis=(0, 2, 3))
    faded = pinned((dy * entry).astype(low))
    direct = mm("cet,ctn->cen", flatten(faded), cmat).reshape(count, H, P_SIZE, N)
    leaving = [None] * count + [jnp.zeros((H, P_SIZE, N), wide)]
    after = [None] * count + [jnp.ones((H,), wide)]
    for c in reversed(range(count)):
        leaving[c] = leaving[c + 1] * widen(growth[c]) + direct[c]
        after[c] = after[c + 1] * growth[c]
    outflow = incoming(leaving[0].astype(low), -1)
    d_state = jnp.stack([leaving[c + 1] + outflow * widen(after[c + 1]) for c in range(count)])
    d_state_low = d_state.astype(low).reshape(count, E, N)

    dy_low = beside(dy_low, sum_out)
    d_mix = mm("chpt,chps->chts", dy_low, xd_low) * fade
    d_inner = jnp.sum(d_mix, axis=1)
    weight = d_mix * inner[:, None]
    d_cum = jnp.sum(weight, axis=3) - jnp.sum(weight, axis=2) + jnp.sum(dy * from_state, axis=2)
    d_cum = beside(d_cum, sum_out, sum_z)
    pulled = heads(mm("cen,cqn->ceq", d_state_low, bmat)) * tail
    d_xd = mm("chts,chpt->chps", mixing, dy_low) + pulled
    d_xd = beside(d_xd, sum_out, sum_z)
    d_tail = jnp.sum(xd * pulled, axis=2)
    d_keep = growth * jnp.sum(state * d_state, axis=(2, 3))
    d_decay = (
        exact("cht,st->chs", d_cum, upto)
        + exact("chs,st->cht", d_tail, upto - jnp.eye(CHUNK, dtype=wide))
        + d_keep[:, :, None]
    )
    d_delta = jnp.sum(x * d_xd, axis=2) + d_decay * rate[None, :, None]
    d_alog = jnp.sum(d_decay * delta, axis=(0, 2)) * rate
    d_x = turned_back(
        pinned(d_xd * delta[:, :, None, :] + dy * skip32[None, :, None, None])
    )
    d_x = beside(d_x, sum_out, sum_z)
    d_c = mm("cts,csn->ctn", d_inner, bmat) + mm("cet,cen->ctn", flatten(faded), state_low)
    d_b = mm("cts,ctn->csn", d_inner, cmat) + mm("ceq,cen->cqn", flatten(xw), d_state_low)
    d_draw = d_delta.transpose(0, 2, 1).reshape(length, H) * jax.nn.sigmoid(draw)
    d_dt = jnp.sum(d_draw, axis=0)

    d_xc = jnp.concatenate([d_x, d_b.reshape(length, N), d_c.reshape(length, N)], axis=1)
    d_pre = d_xc * silu_parts(pre)[1]
    d_pre = beside(d_pre, sum_out, sum_z)
    d_rim = shifted(d_pre[: taps - 1], "fsdp", -1)
    d_bias = jnp.sum(d_pre, axis=0)
    d_conv = jnp.stack(
        [
            jnp.sum(d_pre * tap_valid(k, 0, length) * full[k : k + length], axis=0)
            for k in range(taps)
        ]
    )
    d_full = jnp.concatenate([d_pre, d_rim], axis=0)
    d_xbc = jnp.zeros_like(xbc)
    for k in range(taps):
        lo = taps - 1 - k
        d_xbc = d_xbc + d_full[lo : lo + length] * conv32[k][None, :] * tap_valid(
            k, lo, lo + length
        )
    d_xbc = beside(d_xbc.astype(low), sum_out, sum_z)
    middle = mixed // 2
    sum_a = Reduction(mm("td,te->de", normed, d_xbc[:, :middle]))
    sum_b = Reduction(mm("td,te->de", normed, d_xbc[:, middle:]), True)
    draw_low = d_draw.astype(low)
    d_in_dt = mm("td,te->de", normed, draw_low)
    d_normed = mm("te,de->td", d_z, w_z)
    d_xbc, d_normed = beside((d_xbc, d_normed), sum_a, sum_b)
    d_normed = d_normed + mm("te,de->td", d_xbc, w_x) + mm("te,de->td", draw_low, w_dt)
    hat_in = u * scale_in
    d_norm = jnp.sum(d_normed * hat_in, axis=0)
    d_hat_in = d_normed * norm32[None, :]
    d_tokens = cotangent.astype(wide) + scale_in * (
        d_hat_in - hat_in * jnp.mean(d_hat_in * hat_in, axis=-1, keepdims=True)
    )

    owned = (d_norm, d_conv.T, d_bias, d_dt, d_alog, d_skip_own, d_gnorm, d_in_dt)
    stacked = jnp.concatenate([v.reshape(ranks, -1) for v in owned], axis=1)
    mine = sum_small(stacked)
    grads, at = [], 0
    for v in smalls:
        grads.append(mine[at : at + v.size].reshape(v.shape))
        at += v.size
    g_norm, g_conv, g_bias, g_dt, g_alog, g_skip, g_gnorm, g_in_dt = grads
    return (
        output,
        d_tokens,
        g_norm,
        jnp.concatenate(
            [sum_z.finish(), sum_a.finish(), sum_b.finish(), g_in_dt], axis=1
        ),
        g_conv.T,
        g_bias,
        g_dt,
        g_alog,
        g_skip,
        g_gnorm,
        sum_out.finish(),
    )


def solution(mesh):
    in_specs = (
        P(("rep", "fsdp"), None),
        P("fsdp"),
        P("fsdp", None),
        P(None, "fsdp"),
        P("fsdp"),
        P("fsdp"),
        P("fsdp"),
        P("fsdp"),
        P("fsdp"),
        P("fsdp", None),
        P("rep"),
        P(("rep", "fsdp"), None),
    )
    out_specs = (
        P(("rep", "fsdp"), None),
        P(("rep", "fsdp"), None),
        P("fsdp"),
        P("fsdp", None),
        P(None, "fsdp"),
        P("fsdp"),
        P("fsdp"),
        P("fsdp"),
        P("fsdp"),
        P("fsdp"),
        P("fsdp", None),
    )
    return jax.shard_map(body, mesh=mesh, in_specs=in_specs, out_specs=out_specs, check_vma=False)
```
